32 devices in a mesh: ctx: 8 (over y, x, core), tp: 4 (over z).
Axes of the slice: x: 2, y: 2, z: 4, core: 2. Of those that a mesh axis runs over, the one named last changes fastest.
Arguments:
- hidden_in: bfloat16 [131072, 1536], P('ctx', 'tp'), may hold values from -6 to 6
- fac_inner: bfloat16 [512, 512], replicated, may hold values from -0.25 to 0.25
- fac_outer: bfloat16 [256, 256], replicated, may hold values from -0.375 to 0.375
- inv_outer: bfloat16 [256, 256], replicated, may hold values from -0.375 to 0.375
- inv_inner: bfloat16 [512, 512], replicated, may hold values from -0.25 to 0.25
- kernel_freq: bfloat16 [256, 512, 1536], P(None, 'ctx', 'tp'), may hold values from -6 to 6
- gate_blocks: bfloat16 [1536, 384], P('tp'), may hold values from -0.3125 to 0.3125
- mix_first: bfloat16 [1536, 384], P('tp'), may hold values from -0.3125 to 0.3125
- mix_second: bfloat16 [1536, 384], P('tp'), may hold values from -0.3125 to 0.3125
- upstream: bfloat16 [131072, 1536], P('ctx', 'tp'), may hold values from -6 to 6
Outputs:
- layer_out: bfloat16 [131072, 1536], P('ctx', 'tp')
- grad_input: bfloat16 [131072, 1536], P('ctx', 'tp')
- grad_kernel: float32 [256, 512, 1536], P(None, 'ctx', 'tp')
- grad_gate: float32 [1536, 384], P('tp', 'ctx')
- grad_first: float32 [1536, 384], P('tp', 'ctx')
- grad_second: float32 [1536, 384], P('tp', 'ctx')
The draws below stay inside these ranges and needn't reach their ends.
All inputs are finite; a program needn't handle non-finite values.
Results may differ from the reference program's by a relative error of at most 0.015.
Values may be sent and summed in bfloat16 or wider, within the bound.
A program may use at most 384 MiB of HBM per device.

```python
import math
import jax
import jax.numpy as jnp
from jax import lax

SEQ = 131072
BLK_B = 512
C = 1536
NBLK = 4
BLK_A = 256
CB = 384


def level_of(rng, shape, shards, low, largest):
    loudness = 1.0
    for axis_at, blocks in shards:
        steps = jax.random.uniform(jax.random.fold_in(jax.random.fold_in(rng, 6), axis_at), (blocks,), jnp.float32, low / len(shards), largest / len(shards))
        loudness = loudness * jnp.repeat(jnp.exp(steps), shape[axis_at] // blocks).reshape((-1,) + (1,) * (len(shape) - 1 - axis_at))
    return loudness


def centred(key, dims, scale, most, pieces=(), kind=jnp.bfloat16):
    drawn = scale * jax.random.normal(key, dims, jnp.float32)
    if pieces:
        drawn = drawn * level_of(key, dims, pieces, -0.22, 0.18)
    return jnp.clip(drawn, -most, most).astype(kind)


def setup_inputs(seed: int = 0) -> dict:
    seeds = jax.random.split(jax.random.key(seed), 11)
    return {
        "hidden_in": centred(seeds[0], (SEQ, C), 1.0, 6.0, ((0, 8), (1, 4))),
        "fac_inner": centred(seeds[1], (BLK_B, BLK_B), BLK_B ** -0.5, 0.25),
        "fac_outer": centred(seeds[2], (BLK_A, BLK_A), BLK_A ** -0.5, 0.375),
        "inv_outer": centred(seeds[3], (BLK_A, BLK_A), BLK_A ** -0.5, 0.375),
        "inv_inner": centred(seeds[4], (BLK_B, BLK_B), BLK_B ** -0.5, 0.25),
        "kernel_freq": centred(seeds[5], (BLK_A, BLK_B, C), 1.0, 6.0, ((1, 8), (2, 4))),
        "gate_blocks": centred(seeds[6], (C, CB), CB ** -0.5, 0.3125, ((0, 4),)),
        "mix_first": centred(seeds[7], (C, CB), CB ** -0.5, 0.3125, ((0, 4),)),
        "mix_second": centred(seeds[8], (C, CB), CB ** -0.5, 0.3125, ((0, 4),)),
        "upstream": centred(seeds[9], (SEQ, C), 1.0, 6.0, ((0, 8), (1, 4))),
    }


def gelu_exact(values):
    return jax.nn.gelu(values, approximate=False)

def widen(values):
    return values.astype(jnp.float32)

def shuffle_forward(matrix):
    row_count = matrix.shape[0]
    return matrix.reshape(row_count, NBLK, CB).transpose(0, 2, 1).reshape(row_count, C)

def shuffle_inverse(matrix):
    row_count = matrix.shape[0]
    return matrix.reshape(row_count, CB, NBLK).transpose(0, 2, 1).reshape(row_count, C)

def split_groups(matrix):
    return matrix.reshape(matrix.shape[0], NBLK, CB).transpose(1, 0, 2)

def join_groups(stacked):
    return stacked.transpose(1, 0, 2).reshape(stacked.shape[1], C)

def token_contract(left, right):
    return lax.dot_general(left, right, (((0,), (0,)), ((), ())), preferred_element_type=jnp.float32)

def right_transposed(left, right):
    return lax.dot_general(left, right, (((1,), (1,)), ((), ())), preferred_element_type=jnp.float32)

def conv_forward(tokens_part, kernel_part, fac_inner, fac_outer, inv_outer, inv_inner):
    cube_input = widen(tokens_part.reshape(BLK_A, BLK_B, CB))
    row_mixed = jnp.einsum('abc,be->aec', cube_input, widen(fac_inner)).astype(jnp.bfloat16)
    spectrum = jnp.einsum('aec,af->fec', widen(row_mixed), widen(fac_outer))
    filtered = (spectrum * widen(kernel_part)).astype(jnp.bfloat16)
    back_mixed = jnp.einsum('fec,fg->gec', widen(filtered), widen(inv_outer)).astype(jnp.bfloat16)
    conv_flat = jnp.einsum('aec,eb->abc', widen(back_mixed), widen(inv_inner)).reshape(SEQ, CB)
    return (spectrum, conv_flat)

def reference(hidden_in, fac_inner, fac_outer, inv_outer, inv_inner, kernel_freq, gate_blocks, mix_first, mix_second, upstream):
    kernel_groups = kernel_freq.reshape(BLK_A, BLK_B, NBLK, CB).transpose(2, 0, 1, 3)
    gate_groups = gate_blocks.reshape(NBLK, CB, CB)
    first_groups = mix_first.reshape(NBLK, CB, CB)
    second_groups = mix_second.reshape(NBLK, CB, CB)
    input_groups = split_groups(hidden_in)
    upstream_groups = split_groups(upstream)

    def front_group(operands):
        tokens_part, kernel_part, gate_part, first_part = operands
        spectrum, conv_flat = conv_forward(tokens_part, kernel_part, fac_inner, fac_outer, inv_outer, inv_inner)
        gate_open = jax.nn.sigmoid(jnp.dot(tokens_part, gate_part, preferred_element_type=jnp.float32))
        mixed = (widen(tokens_part) + gate_open * conv_flat).astype(jnp.bfloat16)
        first_out = jnp.dot(mixed, first_part, preferred_element_type=jnp.float32).astype(jnp.bfloat16)
        return (mixed, first_out)
    mixed_groups, first_outs = lax.map(front_group, (input_groups, kernel_groups, gate_groups, first_groups))
    shuffled = split_groups(shuffle_forward(join_groups(first_outs)))

    def second_group(operands):
        return jnp.dot(operands[0], operands[1], preferred_element_type=jnp.float32).astype(jnp.bfloat16)
    second_out = lax.map(second_group, (shuffled, second_groups))
    merged_wide = widen(shuffle_inverse(join_groups(second_out)))
    mixed_all = join_groups(mixed_groups)
    layer_out = (widen(mixed_all) + gelu_exact(merged_wide)).astype(jnp.bfloat16)
    unused, pull = jax.vjp(gelu_exact, merged_wide)
    grad_merged = pull(widen(upstream))[0].astype(jnp.bfloat16)
    grad_second_out = split_groups(shuffle_forward(grad_merged))

    def second_back(operands):
        shuffled_part, grad_part, second_part = operands
        grad_second = token_contract(shuffled_part, grad_part)
        grad_shuffled = right_transposed(grad_part, second_part).astype(jnp.bfloat16)
        return (grad_second, grad_shuffled)
    grad_seconds, grad_shuffled = lax.map(second_back, (shuffled, grad_second_out, second_groups))
    grad_first_out = split_groups(shuffle_inverse(join_groups(grad_shuffled)))

    def front_back(operands):
        tokens_part, kernel_part, gate_part, first_part, mixed_part, grad_part, upstream_part = operands
        spectrum, conv_flat = conv_forward(tokens_part, kernel_part, fac_inner, fac_outer, inv_outer, inv_inner)
        gate_open = jax.nn.sigmoid(jnp.dot(tokens_part, gate_part, preferred_element_type=jnp.float32))
        grad_first = token_contract(mixed_part, grad_part)
        grad_mixed = widen(upstream_part) + right_transposed(grad_part, first_part)
        grad_conv = (grad_mixed * gate_open).astype(jnp.bfloat16)
        grad_gate_pre = (grad_mixed * conv_flat * gate_open * (1.0 - gate_open)).astype(jnp.bfloat16)
        grad_gate = token_contract(tokens_part, grad_gate_pre)
        gate_back = right_transposed(grad_gate_pre, gate_part)
        grad_back = jnp.einsum('abc,eb->aec', widen(grad_conv.reshape(BLK_A, BLK_B, CB)), widen(inv_inner)).astype(jnp.bfloat16)
        grad_filtered = jnp.einsum('gec,fg->fec', widen(grad_back), widen(inv_outer))
        grad_kernel = grad_filtered * spectrum
        grad_spectrum = (grad_filtered * widen(kernel_part)).astype(jnp.bfloat16)
        grad_row = jnp.einsum('fec,af->aec', widen(grad_spectrum), widen(fac_outer)).astype(jnp.bfloat16)
        conv_back = jnp.einsum('aec,be->abc', widen(grad_row), widen(fac_inner)).reshape(SEQ, CB)
        grad_input = (grad_mixed + gate_back + conv_back).astype(jnp.bfloat16)
        return (grad_input, grad_kernel, grad_gate, grad_first)
    grad_inputs, grad_kernels, grad_gates, grad_firsts = lax.map(front_back, (input_groups, kernel_groups, gate_groups, first_groups, mixed_groups, grad_first_out, upstream_groups))
    loss_scale = 1.0 / math.sqrt(SEQ)
    grad_input = join_groups(grad_inputs)
    grad_kernel = grad_kernels.transpose(1, 2, 0, 3).reshape(BLK_A, BLK_B, C)
    return (layer_out, grad_input, grad_kernel, grad_gates.reshape(C, CB) * loss_scale, grad_firsts.reshape(C, CB) * loss_scale, grad_seconds.reshape(C, CB) * loss_scale)
```

```python
import math

import jax
import jax.numpy as jnp
from jax import lax
from jax.sharding import PartitionSpec as P

PARTS = 4


def gelu_exact(values):
    return jax.nn.gelu(values, approximate=False)


def token_contract(left, right):
    return lax.dot_general(
        left, right, (((0,), (0,)), ((), ())), preferred_element_type=jnp.float32
    )


def right_transposed(left, right):
    return lax.dot_general(
        left, right, (((1,), (1,)), ((), ())), preferred_element_type=jnp.float32
    )


def shifted(values, by):
    group_count = lax.axis_size("tp")
    pairs = [(at, (at + by) % group_count) for at in range(group_count)]
    return lax.ppermute(values, "tp", pairs)


def to_tokens(chunk):
    group_count = lax.axis_size("tp")
    here = lax.axis_index("tp")
    rows = chunk.shape[0] // group_count
    pieces = []
    for by in range(group_count):
        goal = lax.rem(here + by, group_count)
        piece = lax.dynamic_slice_in_dim(chunk, goal * rows, rows, 0)
        pieces.append(piece if by == 0 else shifted(piece, by))
    return jnp.concatenate(pieces, axis=1)


def to_channels(matrix):
    group_count = lax.axis_size("tp")
    here = lax.axis_index("tp")
    rows, width = matrix.shape[0], matrix.shape[1] // group_count
    result = jnp.zeros((rows * group_count, width), matrix.dtype)
    for by in range(group_count):
        piece = matrix[:, by * width : (by + 1) * width]
        if by:
            piece = shifted(piece, group_count - by)
        quarter = lax.rem(here + by, group_count)
        result = lax.dynamic_update_slice_in_dim(result, piece, quarter * rows, 0)
    return result


def turned(values, axis):
    group_count = lax.axis_size("tp")
    here = lax.axis_index("tp")
    blocks = [
        lax.dynamic_slice_in_dim(values, lax.rem(here - by + group_count, group_count), 1, axis)
        for by in range(group_count)
    ]
    return jnp.concatenate(blocks, axis=axis)


def spread_second(mix_second):
    width = mix_second.shape[0]
    group_count = lax.axis_size("tp")
    piece = width // group_count
    second_rows = (
        mix_second.reshape(piece, group_count, width).transpose(1, 0, 2).reshape(width, width)
    )
    second_local = (
        second_rows.reshape(width, piece, group_count).transpose(0, 2, 1).reshape(width, width)
    )
    blocks = lax.all_gather(second_local, "tp", axis=0, tiled=False)
    blocks = blocks.reshape(group_count, group_count, piece, group_count, piece)
    blocks = turned(turned(blocks, 1), 3)
    parts = []
    for k in range(group_count):
        gaps = ((0, 0), (0, 0), (0, 0), (k * piece, width - (k + 1) * piece))
        parts.append(jnp.pad(blocks[k], gaps))
    whole = group_count * width
    return jnp.concatenate(parts, axis=1).reshape(whole, whole)


def gather_second(full):
    group_count = lax.axis_size("tp")
    width = full.shape[0] // group_count
    piece = width // group_count
    cube = full.reshape(group_count, width, group_count, width)
    blocks = jnp.stack(
        [
            cube[:, k * piece : (k + 1) * piece, :, k * piece : (k + 1) * piece]
            for k in range(group_count)
        ]
    )
    blocks = turned(turned(blocks, 1), 3).reshape(group_count * width, width)
    local_sum = lax.psum_scatter(blocks, "tp", scatter_dimension=0, tiled=True)
    unrow = (
        local_sum.reshape(group_count, piece, width).transpose(1, 0, 2).reshape(width, width)
    )
    return unrow.reshape(width, group_count, piece).transpose(0, 2, 1).reshape(width, width)


def chunk_order(matrix, axis, parts):
    devices = lax.axis_size("ctx")
    moved = jnp.moveaxis(matrix, axis, 0)
    length, other = moved.shape
    rows = length // (devices * parts)
    moved = moved.reshape(devices, parts, rows, other).transpose(1, 0, 2, 3)
    return jnp.moveaxis(moved.reshape(length, other), 0, axis)


def local(
    hidden_in,
    fac_inner,
    fac_outer,
    inv_outer,
    inv_inner,
    kernel_freq,
    gate_blocks,
    mix_first,
    mix_second,
    upstream,
):
    tok_rows, local_width = hidden_in.shape
    inner_len = fac_inner.shape[0]
    outer_len = fac_outer.shape[0]
    local_outer = tok_rows // inner_len
    parts = min(PARTS, local_outer)
    part_outer = local_outer // parts
    part_rows = tok_rows // parts
    part_span = outer_len // parts

    def rows_of(matrix, part):
        return matrix[part * part_rows : (part + 1) * part_rows]

    second_full = spread_second(mix_second)
    inv_outer_parts = chunk_order(inv_outer, 1, parts)
    fac_outer_parts = chunk_order(fac_outer, 0, parts)

    up_tokens = [to_tokens(rows_of(upstream, part)) for part in range(parts)]

    cube_input = hidden_in.reshape(local_outer, inner_len, local_width)
    row_mixed = jnp.einsum(
        "abc,be->aec", cube_input, fac_inner, preferred_element_type=jnp.float32
    ).astype(jnp.bfloat16)
    columns = lax.all_to_all(row_mixed, "ctx", split_axis=1, concat_axis=0, tiled=True)
    spectrum = jnp.einsum("aec,af->fec", columns, fac_outer, preferred_element_type=jnp.float32)
    kernel_wide = kernel_freq.astype(jnp.float32)
    filtered = (spectrum * kernel_wide).astype(jnp.bfloat16)
    back_mixed = jnp.einsum(
        "fec,fg->gec", filtered, inv_outer_parts, preferred_element_type=jnp.float32
    ).astype(jnp.bfloat16)
    back_mixed, up_tokens = lax.optimization_barrier((back_mixed, up_tokens))

    gates, convs, mixes, firsts, mergeds = [], [], [], [], []
    slopes, grad_firsts = [], []
    for part in range(parts):
        returned = lax.all_to_all(
            back_mixed[part * part_span : (part + 1) * part_span],
            "ctx",
            split_axis=0,
            concat_axis=1,
            tiled=True,
        )
        conv_flat = jnp.einsum(
            "aec,eb->abc", returned, inv_inner, preferred_element_type=jnp.float32
        ).reshape(part_rows, local_width)
        tokens = rows_of(hidden_in, part)
        gate_open = jax.nn.sigmoid(jnp.dot(tokens, gate_blocks, preferred_element_type=jnp.float32))
        mixed = (tokens.astype(jnp.float32) + gate_open * conv_flat).astype(jnp.bfloat16)
        first_out = jnp.dot(mixed, mix_first, preferred_element_type=jnp.float32).astype(
            jnp.bfloat16
        )
        gates.append(gate_open)
        convs.append(conv_flat)
        mixes.append(mixed)
        firsts.append(to_tokens(first_out))
    for part in range(parts):
        merged = jnp.dot(firsts[part], second_full, preferred_element_type=jnp.float32).astype(
            jnp.bfloat16
        )
        unused, pull = jax.vjp(gelu_exact, merged.astype(jnp.float32))
        grad_merged = pull(up_tokens[part].astype(jnp.float32))[0].astype(jnp.bfloat16)
        grad_shuffled = right_transposed(grad_merged, second_full).astype(jnp.bfloat16)
        mergeds.append(merged)
        slopes.append(grad_merged)
        grad_firsts.append(to_channels(grad_shuffled))

    grad_first = 0.0
    grad_gate = 0.0
    bases, grad_columns = [], []
    for part in range(parts):
        grad_first = grad_first + token_contract(mixes[part], grad_firsts[part])
        grad_mixed = rows_of(upstream, part).astype(jnp.float32) + right_transposed(
            grad_firsts[part], mix_first
        )
        gate_open, conv_flat = gates[part], convs[part]
        grad_conv = (grad_mixed * gate_open).astype(jnp.bfloat16)
        grad_gate_pre = (grad_mixed * conv_flat * gate_open * (1.0 - gate_open)).astype(
            jnp.bfloat16
        )
        grad_gate = grad_gate + token_contract(rows_of(hidden_in, part), grad_gate_pre)
        bases.append(grad_mixed + right_transposed(grad_gate_pre, gate_blocks))
        grad_back = jnp.einsum(
            "abc,eb->aec",
            grad_conv.reshape(part_outer, inner_len, local_width),
            inv_inner,
            preferred_element_type=jnp.float32,
        ).astype(jnp.bfloat16)
        grad_columns.append(
            lax.all_to_all(grad_back, "ctx", split_axis=1, concat_axis=0, tiled=True)
        )
    mergeds, tied = lax.optimization_barrier((mergeds, grad_firsts[-1]))
    layer_out = jnp.concatenate(
        [
            (
                mixes[part].astype(jnp.float32)
                + gelu_exact(to_channels(mergeds[part]).astype(jnp.float32))
            ).astype(jnp.bfloat16)
            for part in range(parts)
        ]
    )
    grad_filtered = jnp.einsum(
        "gec,fg->fec",
        jnp.concatenate(grad_columns),
        inv_outer_parts,
        preferred_element_type=jnp.float32,
    )
    grad_kernel = grad_filtered * spectrum
    grad_spectrum = (grad_filtered * kernel_wide).astype(jnp.bfloat16)
    grad_row = jnp.einsum(
        "fec,af->aec", grad_spectrum, fac_outer_parts, preferred_element_type=jnp.float32
    ).astype(jnp.bfloat16)
    inputs = []
    for part in range(parts):
        grad_cube = lax.all_to_all(
            grad_row[part * part_span : (part + 1) * part_span],
            "ctx",
            split_axis=0,
            concat_axis=1,
            tiled=True,
        )
        conv_back = jnp.einsum(
            "aec,be->abc", grad_cube, fac_inner, preferred_element_type=jnp.float32
        ).reshape(part_rows, local_width)
        inputs.append((bases[part] + conv_back).astype(jnp.bfloat16))
    grad_input = jnp.concatenate(inputs)
    second_product = 0.0
    for part in range(parts):
        second_product = second_product + token_contract(firsts[part], slopes[part])
    grad_second = gather_second(second_product)
    loss_scale = 1.0 / math.sqrt(tok_rows * lax.axis_size("ctx"))
    summed = (
        lax.psum_scatter(grad_gate * loss_scale, "ctx", scatter_dimension=1, tiled=True),
        lax.psum_scatter(grad_first * loss_scale, "ctx", scatter_dimension=1, tiled=True),
        lax.psum_scatter(grad_second * loss_scale, "ctx", scatter_dimension=1, tiled=True),
    )
    return (layer_out, grad_input, grad_kernel, summed[0], summed[1], summed[2])


def solution(mesh):
    placed = (
        P("ctx", "tp"),
        P(),
        P(),
        P(),
        P(),
        P(None, "ctx", "tp"),
        P("tp", None),
        P("tp", None),
        P("tp", None),
        P("ctx", "tp"),
    )
    return jax.shard_map(
        local,
        mesh=mesh,
        in_specs=placed,
        out_specs=(
            P("ctx", "tp"),
            P("ctx", "tp"),
            P(None, "ctx", "tp"),
            P("tp", "ctx"),
            P("tp", "ctx"),
            P("tp", "ctx"),
        ),
        check_vma=False,
    )
```
